32 devices in a mesh: job: 2 (over x), fsdp: 16 (over z, y, core).
Axes of the slice: x: 2, y: 2, z: 4, core: 2. Of those that a mesh axis runs over, the one named last changes fastest.
Arguments:
- decode_input_rows: bfloat16 [32, 2, 5120], P(('job', 'fsdp')), parts along dimension 0, may hold values from -150 to 150
- cached_rotated_keys: bfloat16 [32, 2048, 1024], P(('job', 'fsdp')), parts along dimension 0, may hold values from -4 to 4
- cached_value_rows: bfloat16 [32, 2048, 1024], P(('job', 'fsdp')), parts along dimension 0, may hold values from -5 to 5
- lengths: int32 [32], P(('job', 'fsdp')), parts along dimension 0, may hold values from 1 to 2048, as said below
- base_query_weight: bfloat16 [5120, 8192], P(None, 'fsdp'), may hold values from -0.078125 to 0.078125
- base_key_weight: bfloat16 [5120, 1024], P(None, 'fsdp'), may hold values from -0.078125 to 0.078125
- base_value_weight: bfloat16 [5120, 1024], P(None, 'fsdp'), may hold values from -0.078125 to 0.078125
- base_output_weight: bfloat16 [8192, 5120], P('fsdp'), may hold values from -1.5 to 1.5
- query_adapter_down: bfloat16 [10240, 64], P(('job', 'fsdp')), parts along dimension 0, may hold values from -0.75 to 0.75
- query_adapter_up: bfloat16 [16384, 64], P(('job', 'fsdp')), parts along dimension 0, may hold values from -0.0390625 to 0.0390625
- key_adapter_down: bfloat16 [10240, 64], P(('job', 'fsdp')), parts along dimension 0, may hold values from -0.75 to 0.75
- key_adapter_up: bfloat16 [2048, 64], P(('job', 'fsdp')), parts along dimension 0, may hold values from -0.0390625 to 0.0390625
- value_adapter_down: bfloat16 [10240, 64], P(('job', 'fsdp')), parts along dimension 0, may hold values from -0.75 to 0.75
- value_adapter_up: bfloat16 [2048, 64], P(('job', 'fsdp')), parts along dimension 0, may hold values from -0.0390625 to 0.0390625
- output_adapter_down: bfloat16 [16384, 64], P(('job', 'fsdp')), parts along dimension 0, may hold values from -0.75 to 0.75
- output_adapter_up: bfloat16 [10240, 64], P(('job', 'fsdp')), parts along dimension 0, may hold values from -0.375 to 0.375
Outputs:
- block_out: bfloat16 [32, 2, 5120], P(('job', 'fsdp')), parts along dimension 0
- new_keys: bfloat16 [32, 2, 1024], P(('job', 'fsdp')), parts along dimension 0
- new_values: bfloat16 [32, 2, 1024], P(('job', 'fsdp')), parts along dimension 0
The draws below stay inside these ranges and needn't reach their ends.
There are 2 independent parts, one for each index of `job`. The reference program is written for one: setup_inputs(seed, part) draws one part's arguments, and reference() takes and returns one part's arrays. A program takes and returns all parts, laid end to end along the dimension named above; an argument that names none is the same for every part. Nothing has to cross between parts.
Inputs may be any that keep to these rules, and one draw needn't show every extreme that they name: Row r's cache holds keys and values at positions 0 to lengths[r] - 1, other positions hold unrelated numbers; some row has exactly 2048 and some row exactly 1.
All inputs are finite; a program needn't handle non-finite values.
Results may differ from the reference program's by a relative error of at most 0.014.
Values may be sent and summed in bfloat16 or wider, within the bound.
A program may use at most 128 MiB of HBM per device.

```python
import math
import jax
import jax.numpy as jnp
from jax import lax

MODEL_WIDTH = 5120
QHEADS = 64
KVHEADS = 8
HEAD = 128
ADAPTER_RANK = 64
STEPS = 2
LMAX = 2048
ROWS = 16
QUERY_FEATURES = 8192
KEY_FEATURES = 1024


def draw_decode_input_rows(key, part):
    key = jax.random.fold_in(key, 11)
    key_cols, key_base = jax.random.split(key, 2)
    columns = jnp.exp(jax.random.uniform(key_cols, (MODEL_WIDTH,), jnp.float32, 0.0, math.log(10.0)))
    values = jnp.clip(jax.random.normal(key_base, (ROWS, STEPS, MODEL_WIDTH), jnp.float32), -5.0, 5.0) * columns
    return values.astype(jnp.bfloat16)


def draw_lengths(key, part):
    key = jax.random.fold_in(key, 23)
    key_values, key_order = jax.random.split(key)
    values = jax.random.randint(key_values, (ROWS,), 1, LMAX + 1)
    order = jax.random.permutation(key_order, ROWS)
    values = values.at[order[0]].set(LMAX)
    values = values.at[order[1]].set(1)
    return values.astype(jnp.int32)


def block_levels(rng, dims, pieces, low, largest):
    def one(axis_at, blocks):
        steps = jax.random.uniform(jax.random.fold_in(jax.random.fold_in(rng, 6), axis_at), (blocks,), jnp.float32, low / len(pieces), largest / len(pieces))
        return jnp.repeat(jnp.exp(steps), dims[axis_at] // blocks).reshape((-1,) + (1,) * (len(dims) - axis_at - 1))

    factor_of = one(*pieces[0])
    for cut in pieces[1:]:
        factor_of = factor_of * one(*cut)
    return factor_of


def normal_values(own_key, shape, scale, most, cuts=(), held_as=jnp.bfloat16):
    level = block_levels(own_key, shape, cuts, -0.22, 0.18) if cuts else 1.0
    array = jax.random.normal(own_key, shape, jnp.float32) * scale * level
    return jnp.minimum(jnp.maximum(array, -most), most).astype(held_as)


def setup_inputs(seed: int = 0, part: int = 0) -> dict:
    streams_of = jax.random.split(jax.random.key(seed), 17)
    own_keys = jax.random.split(jax.random.fold_in(streams_of[16], part), 17)
    return {
        "decode_input_rows": draw_decode_input_rows(jax.random.fold_in(jax.random.fold_in(streams_of[16], part), 71), part),
        "cached_rotated_keys": normal_values(own_keys[1], (ROWS, LMAX, KEY_FEATURES), 1.0, 4.0, ((0, 16),)),
        "cached_value_rows": normal_values(own_keys[2], (ROWS, LMAX, KEY_FEATURES), 1.0, 5.0, ((0, 16),)),
        "lengths": draw_lengths(jax.random.fold_in(jax.random.fold_in(streams_of[16], part), 71), part),
        "base_query_weight": normal_values(streams_of[4], (MODEL_WIDTH, QUERY_FEATURES), MODEL_WIDTH ** -0.5, 0.078125, ((1, 16),)),
        "base_key_weight": normal_values(streams_of[5], (MODEL_WIDTH, KEY_FEATURES), MODEL_WIDTH ** -0.5, 0.078125, ((1, 16),)),
        "base_value_weight": normal_values(streams_of[6], (MODEL_WIDTH, KEY_FEATURES), MODEL_WIDTH ** -0.5, 0.078125, ((1, 16),)),
        "base_output_weight": normal_values(streams_of[7], (QUERY_FEATURES, MODEL_WIDTH), 16 ** -0.5, 1.5, ((0, 16),)),
        "query_adapter_down": normal_values(own_keys[8], (MODEL_WIDTH, ADAPTER_RANK), ADAPTER_RANK ** -0.5, 0.75, ((0, 16),)),
        "query_adapter_up": normal_values(own_keys[9], (QUERY_FEATURES, ADAPTER_RANK), (4 * MODEL_WIDTH) ** -0.5, 0.0390625, ((0, 16),)),
        "key_adapter_down": normal_values(own_keys[10], (MODEL_WIDTH, ADAPTER_RANK), ADAPTER_RANK ** -0.5, 0.75, ((0, 16),)),
        "key_adapter_up": normal_values(own_keys[11], (KEY_FEATURES, ADAPTER_RANK), (4 * MODEL_WIDTH) ** -0.5, 0.0390625, ((0, 16),)),
        "value_adapter_down": normal_values(own_keys[12], (MODEL_WIDTH, ADAPTER_RANK), ADAPTER_RANK ** -0.5, 0.75, ((0, 16),)),
        "value_adapter_up": normal_values(own_keys[13], (KEY_FEATURES, ADAPTER_RANK), (4 * MODEL_WIDTH) ** -0.5, 0.0390625, ((0, 16),)),
        "output_adapter_down": normal_values(own_keys[14], (QUERY_FEATURES, ADAPTER_RANK), ADAPTER_RANK ** -0.5, 0.75, ((0, 16),)),
        "output_adapter_up": normal_values(own_keys[15], (MODEL_WIDTH, ADAPTER_RANK), 256 ** -0.5, 0.375, ((0, 16),)),
    }


SCALE = 2.0
THETA = 1000000.0
EPSILON = 1e-06

def combined_weight_matrix(base, left, right):
    delta = jnp.dot(left, right.T, preferred_element_type=jnp.float32)
    return (base.astype(jnp.float32) + SCALE * delta).astype(jnp.bfloat16)

def rms_rows(values):
    wide = values.astype(jnp.float32)
    return wide * lax.rsqrt(lax.optimization_barrier(jnp.mean(wide * wide, axis=-1, keepdims=True)) + EPSILON)

def rotary(heads, positions):
    half_size = heads.shape[-1] // 2
    frequency = THETA ** (-2.0 * jnp.arange(half_size, dtype=jnp.float32) / heads.shape[-1])
    angles = positions.astype(jnp.float32)[:, None] * frequency[None, :]
    cosine = jnp.cos(angles)[:, None, :]
    sine_part = jnp.sin(angles)[:, None, :]
    first = heads[..., :half_size]
    second = heads[..., half_size:]
    return jnp.concatenate([first * cosine - second * sine_part, second * cosine + first * sine_part], axis=-1)

def attend_row(query_rot, keys, values, valid, fresh_keys, fresh_values):
    group = QHEADS // KVHEADS
    query = query_rot.astype(jnp.float32).reshape(KVHEADS, group, HEAD)
    cached_k = keys.astype(jnp.float32).reshape(LMAX, KVHEADS, HEAD)
    cached_v = values.astype(jnp.float32).reshape(LMAX, KVHEADS, HEAD)
    recent_k = fresh_keys.astype(jnp.float32).reshape(-1, KVHEADS, HEAD)
    recent_v = fresh_values.astype(jnp.float32).reshape(-1, KVHEADS, HEAD)
    scores = jnp.einsum('gqd,lgd->gql', query, cached_k) / math.sqrt(HEAD)
    fresh_scores = jnp.einsum('gqd,lgd->gql', query, recent_k) / math.sqrt(HEAD)
    weights = jnp.where(valid[None, None, :], jnp.exp(scores), jnp.float32(0.0))
    fresh_weights = jnp.exp(fresh_scores)
    total = lax.optimization_barrier(jnp.sum(weights, axis=-1, keepdims=True)) + lax.optimization_barrier(jnp.sum(fresh_weights, axis=-1, keepdims=True))
    shares = (weights / total).astype(jnp.bfloat16).astype(jnp.float32)
    fresh_shares = (fresh_weights / total).astype(jnp.bfloat16).astype(jnp.float32)
    mixed = jnp.einsum('gql,lgd->gqd', shares, cached_v) + jnp.einsum('gql,lgd->gqd', fresh_shares, recent_v)
    return mixed.reshape(QUERY_FEATURES).astype(jnp.bfloat16)

def reference(decode_input_rows, cached_rotated_keys, cached_value_rows, lengths, base_query_weight, base_key_weight, base_value_weight, base_output_weight, query_adapter_down, query_adapter_up, key_adapter_down, key_adapter_up, value_adapter_down, value_adapter_up, output_adapter_down, output_adapter_up):
    combined_query_weight = combined_weight_matrix(base_query_weight, query_adapter_down, query_adapter_up)
    combined_key_weight = combined_weight_matrix(base_key_weight, key_adapter_down, key_adapter_up)
    combined_value_weight = combined_weight_matrix(base_value_weight, value_adapter_down, value_adapter_up)
    combined_output_weight = combined_weight_matrix(base_output_weight, output_adapter_down, output_adapter_up)
    valid = jnp.arange(LMAX, dtype=jnp.int32)[None, :] < lengths[:, None]
    fresh_keys = []
    fresh_values = []
    results = []
    for step in range(STEPS):
        stream = decode_input_rows[:, step].astype(jnp.float32)
        if step > 0:
            stream = stream + results[-1].astype(jnp.float32)
        normed = rms_rows(stream).astype(jnp.bfloat16)
        query = jnp.dot(normed, combined_query_weight, preferred_element_type=jnp.float32).astype(jnp.bfloat16)
        key = jnp.dot(normed, combined_key_weight, preferred_element_type=jnp.float32).astype(jnp.bfloat16)
        value = jnp.dot(normed, combined_value_weight, preferred_element_type=jnp.float32).astype(jnp.bfloat16)
        positions = lengths + step
        query_rot = rotary(rms_rows(query.reshape(ROWS, QHEADS, HEAD)), positions).astype(jnp.bfloat16)
        key_rot = rotary(rms_rows(key.reshape(ROWS, KVHEADS, HEAD)), positions).astype(jnp.bfloat16)
        fresh_keys.append(key_rot.reshape(ROWS, KEY_FEATURES))
        fresh_values.append(value)
        stacked_k = jnp.stack(fresh_keys, axis=1)
        stacked_v = jnp.stack(fresh_values, axis=1)
        mixed = lax.map(lambda item: attend_row(*item), (query_rot.reshape(ROWS, QUERY_FEATURES), cached_rotated_keys, cached_value_rows, valid, stacked_k, stacked_v))
        results.append(jnp.dot(mixed, combined_output_weight, preferred_element_type=jnp.float32).astype(jnp.bfloat16))
    return (jnp.stack(results, axis=1), jnp.stack(fresh_keys, axis=1), jnp.stack(fresh_values, axis=1))
```

```python
import functools
import math

import jax
import jax.numpy as jnp
from jax import lax
from jax.experimental import pallas as pl
from jax.experimental.pallas import tpu as pltpu
from jax.sharding import PartitionSpec as P

QHEADS = 64
KVHEADS = 8
HEAD = 128
STEPS = 2


SCALE = 2.0
THETA = 1000000.0
EPSILON = 1e-06


def combined_weight_matrix(base, left, right):
    delta = jnp.dot(left, right.T, preferred_element_type=jnp.float32)
    return (base.astype(jnp.float32) + SCALE * delta).astype(jnp.bfloat16)


def rms_rows(values):
    wide = values.astype(jnp.float32)
    return wide * lax.rsqrt(jnp.mean(wide * wide, axis=-1, keepdims=True) + EPSILON)


def rotary(heads, positions):
    half_size = heads.shape[-1] // 2
    frequency = THETA ** (-2.0 * jnp.arange(half_size, dtype=jnp.float32) / heads.shape[-1])
    angles = positions.astype(jnp.float32)[:, None] * frequency[None, :]
    cosine = jnp.cos(angles)[:, None, :]
    sine_part = jnp.sin(angles)[:, None, :]
    first = heads[..., :half_size]
    second = heads[..., half_size:]
    return jnp.concatenate(
        [first * cosine - second * sine_part, second * cosine + first * sine_part], axis=-1
    )


def attend(query_rot, cached_rotated_keys, cached_value_rows, valid, fresh_keys, fresh_values):
    rows_here, length, width = cached_rotated_keys.shape
    groups = width // HEAD
    query = query_rot.reshape(rows_here, groups, -1, HEAD)
    cached_k = cached_rotated_keys.reshape(rows_here, length, groups, HEAD)
    cached_v = cached_value_rows.reshape(rows_here, length, groups, HEAD)
    recent_k = fresh_keys.reshape(rows_here, -1, groups, HEAD)
    recent_v = fresh_values.reshape(rows_here, -1, groups, HEAD)
    scores = jnp.einsum(
        "rgqd,rlgd->rgql", query, cached_k, preferred_element_type=jnp.float32
    ) / math.sqrt(HEAD)
    fresh_scores = jnp.einsum(
        "rgqd,rlgd->rgql", query, recent_k, preferred_element_type=jnp.float32
    ) / math.sqrt(HEAD)
    weights = jnp.where(valid[:, None, None, :], jnp.exp(scores), jnp.float32(0.0))
    fresh_weights = jnp.exp(fresh_scores)
    total = jnp.sum(weights, axis=-1, keepdims=True) + jnp.sum(
        fresh_weights, axis=-1, keepdims=True
    )
    shares = (weights / total).astype(jnp.bfloat16)
    fresh_shares = (fresh_weights / total).astype(jnp.bfloat16)
    mixed = jnp.einsum("rgql,rlgd->rgqd", shares, cached_v, preferred_element_type=jnp.float32)
    mixed = mixed + jnp.einsum(
        "rgql,rlgd->rgqd", fresh_shares, recent_v, preferred_element_type=jnp.float32
    )
    return mixed.reshape(rows_here, -1).astype(jnp.bfloat16)


def per_device_plain(
    decode_input_rows,
    cached_rotated_keys,
    cached_value_rows,
    lengths,
    base_query_weight,
    base_key_weight,
    base_value_weight,
    base_output_weight,
    query_adapter_down,
    query_adapter_up,
    key_adapter_down,
    key_adapter_up,
    value_adapter_down,
    value_adapter_up,
    output_adapter_down,
    output_adapter_up,
):
    expanded_query_down, expanded_key_down, expanded_value_down, complete_output_rows = (
        lax.all_gather(query_adapter_down, "fsdp", axis=0, tiled=True),
        lax.all_gather(key_adapter_down, "fsdp", axis=0, tiled=True),
        lax.all_gather(value_adapter_down, "fsdp", axis=0, tiled=True),
        lax.all_gather(output_adapter_up, "fsdp", axis=0, tiled=True),
    )
    combined_query_weight = combined_weight_matrix(
        base_query_weight, expanded_query_down, query_adapter_up
    )
    combined_key_weight = combined_weight_matrix(base_key_weight, expanded_key_down, key_adapter_up)
    combined_value_weight = combined_weight_matrix(
        base_value_weight, expanded_value_down, value_adapter_up
    )
    combined_output_weight = combined_weight_matrix(
        base_output_weight, output_adapter_down, complete_output_rows
    )
    rows_here = decode_input_rows.shape[0]
    valid = jnp.arange(cached_rotated_keys.shape[1], dtype=jnp.int32)[None, :] < lengths[:, None]
    fresh_keys = []
    fresh_values = []
    results = []
    for step in range(STEPS):
        stream = decode_input_rows[:, step].astype(jnp.float32)
        if step > 0:
            stream = stream + results[-1].astype(jnp.float32)
        normed = rms_rows(stream).astype(jnp.bfloat16)
        gathered = lax.all_gather(normed, "fsdp", axis=0, tiled=True)
        query = jnp.dot(gathered, combined_query_weight, preferred_element_type=jnp.float32).astype(
            jnp.bfloat16
        )
        key = jnp.dot(gathered, combined_key_weight, preferred_element_type=jnp.float32).astype(
            jnp.bfloat16
        )
        value = jnp.dot(gathered, combined_value_weight, preferred_element_type=jnp.float32).astype(
            jnp.bfloat16
        )
        query, key, value = (
            lax.all_to_all(query, "fsdp", split_axis=0, concat_axis=1, tiled=True),
            lax.all_to_all(key, "fsdp", split_axis=0, concat_axis=1, tiled=True),
            lax.all_to_all(value, "fsdp", split_axis=0, concat_axis=1, tiled=True),
        )
        positions = lengths + step
        query_rot = rotary(rms_rows(query.reshape(rows_here, QHEADS, HEAD)), positions).astype(
            jnp.bfloat16
        )
        key_rot = rotary(rms_rows(key.reshape(rows_here, KVHEADS, HEAD)), positions).astype(
            jnp.bfloat16
        )
        fresh_keys.append(key_rot.reshape(rows_here, -1))
        fresh_values.append(value)
        mixed = attend(
            query_rot,
            cached_rotated_keys,
            cached_value_rows,
            valid,
            jnp.stack(fresh_keys, axis=1),
            jnp.stack(fresh_values, axis=1),
        )
        spread = lax.all_to_all(mixed, "fsdp", split_axis=1, concat_axis=0, tiled=True)
        result = lax.psum_scatter(
            jnp.dot(spread, combined_output_weight, preferred_element_type=jnp.float32),
            "fsdp",
            scatter_dimension=0,
            tiled=True,
        )
        results.append(result.astype(jnp.bfloat16))
    return (
        jnp.stack(results, axis=1),
        jnp.stack(fresh_keys, axis=1),
        jnp.stack(fresh_values, axis=1),
    )


SLOT = 8
PIECES = 16


def decode_kernel(
    n,
    length_ref,
    x_ref,
    trig_ref,
    keys_hbm,
    values_hbm,
    wq_hbm,
    wk_hbm,
    wv_hbm,
    wo_hbm,
    dq_ref,
    dk_ref,
    dv_ref,
    uq_ref,
    uk_ref,
    uv_ref,
    do_ref,
    uo_ref,
    out_ref,
    newk_ref,
    newv_ref,
    keys,
    values,
    wq,
    wk,
    wv,
    wo,
    row_send,
    rows_got,
    wide,
    xmat,
    low_send,
    low_got,
    head_send,
    head_got,
    mix_send,
    mix_got,
    mid_send,
    mid_got,
    part_send,
    part_got,
    load_sem,
    send_sem,
    recv_sem,
):
    me = lax.axis_index("fsdp")
    chunks = x_ref.shape[1]
    padded = rows_got.shape[1]
    depth = xmat.shape[2]
    share = dq_ref.shape[0]
    rank = dq_ref.shape[1]
    half = HEAD // 2
    own_heads = wq.shape[1] // HEAD
    length = keys.shape[0]
    group = QHEADS // KVHEADS

    loads = [
        pltpu.make_async_copy(source, target, load_sem.at[i])
        for i, (source, target) in enumerate(
            (
                (wq_hbm, wq),
                (wk_hbm, wk),
                (wv_hbm, wv),
                (keys_hbm, keys),
                (values_hbm, values),
                (wo_hbm, wo),
            )
        )
    ]
    for load in loads:
        load.start()

    barrier = pltpu.get_barrier_semaphore()

    def greet(i, carry):
        pl.semaphore_signal(
            barrier,
            inc=1,
            device_id={"fsdp": lax.rem(me + i, n)},
            device_id_type=pl.DeviceIdType.MESH,
        )
        return carry

    lax.fori_loop(1, n, greet, 0)
    head_send[...] = jnp.zeros_like(head_send)
    mix_send[...] = jnp.zeros_like(mix_send)
    newk_ref[...] = jnp.zeros_like(newk_ref)
    newv_ref[...] = jnp.zeros_like(newv_ref)
    part_got[...] = jnp.zeros_like(part_got)
    pl.semaphore_wait(barrier, n - 1)

    def exchange(which, source_of, target):
        def send(i, carry):
            peer = lax.rem(me + i, n)
            pltpu.make_async_remote_copy(
                src_ref=source_of(peer),
                dst_ref=target.at[me],
                send_sem=send_sem.at[which],
                recv_sem=recv_sem.at[which],
                device_id={"fsdp": peer},
                device_id_type=pl.DeviceIdType.MESH,
            ).start()
            return carry

        lax.fori_loop(1, n, send, 0)

    def arrive(which, target):
        whole = target.at[pl.ds(0, n - 1)]
        pltpu.make_async_copy(whole, whole, recv_sem.at[which]).wait()
        pltpu.make_async_copy(whole, whole, send_sem.at[which]).wait()

    odd = lax.rem(me, 2)
    first_chunk = 5 * (me // 2) + 2 * odd
    lane = lax.broadcasted_iota(jnp.int32, (KVHEADS, HEAD), 1)

    def step_body(step, carry):
        stream = x_ref[step] + jnp.sum(part_got[...].astype(jnp.float32), axis=0)[
            :chunks
        ].astype(jnp.bfloat16).astype(jnp.float32)
        mean = jnp.sum(jnp.sum(stream * stream, axis=1, keepdims=True), axis=0, keepdims=True) / (
            chunks * HEAD
        )
        normed = stream * lax.rsqrt(mean + EPSILON)
        normed = jnp.concatenate(
            [normed, jnp.zeros((padded - chunks, HEAD), jnp.float32)], axis=0
        ).astype(jnp.bfloat16)
        row_send[...] = normed
        rows_got[me] = normed
        exchange(0, lambda peer: row_send, rows_got)
        arrive(0, rows_got)
        for r in range(n):
            wide[pl.ds(r * padded, padded), :] = rows_got[r].astype(jnp.float32)
        mine = [
            wide[pl.ds(first_chunk + j, n, stride=padded), :] for j in range(3)
        ]
        mine = jnp.concatenate(mine, axis=1)
        mine = jnp.where(odd == 1, mine[:, half : half + share], mine[:, :share]).astype(
            jnp.bfloat16
        )
        low = [
            jnp.dot(mine, ref[...], preferred_element_type=jnp.float32)
            for ref in (dq_ref, dk_ref, dv_ref)
        ]
        low = jnp.concatenate(low + [jnp.zeros((n, rank), jnp.float32)], axis=1).astype(
            jnp.bfloat16
        )
        low_send[...] = low
        low_got[me] = low
        exchange(1, lambda peer: low_send, low_got)
        per = depth // HEAD
        for c in range(chunks):
            xmat[c // per, :, pl.ds((c % per) * HEAD, HEAD)] = wide[
                pl.ds(c, n, stride=padded), :
            ].astype(jnp.bfloat16)

        @pl.when(step == 0)
        def _():
            for load in loads[:3]:
                load.wait()

        def project(i, sums):
            rows = pl.ds(pl.multiple_of(i * depth, depth), depth)
            left = xmat[i]
            return tuple(
                total + jnp.dot(left, ref[rows, :], preferred_element_type=jnp.float32)
                for total, ref in zip(sums, (wq, wk, wv))
            )

        query, key, value = lax.fori_loop(
            0,
            xmat.shape[0],
            project,
            tuple(jnp.zeros((n, ref.shape[1]), jnp.float32) for ref in (wq, wk, wv)),
        )
        arrive(1, low_got)
        low = jnp.sum(low_got[...].astype(jnp.float32), axis=0).astype(jnp.bfloat16)

        def raised(index, ref):
            return SCALE * lax.dot_general(
                low[:, index * rank : (index + 1) * rank],
                ref[...],
                (((1,), (1,)), ((), ())),
                preferred_element_type=jnp.float32,
            )

        query = query + raised(0, uq_ref)
        pair = jnp.concatenate([key + raised(1, uk_ref), value + raised(2, uv_ref)], axis=1)
        for j in range(own_heads):
            head_send[pl.ds(j, n, stride=SLOT), :] = query[:, j * HEAD : (j + 1) * HEAD]
        head_send[pl.ds(own_heads, n, stride=SLOT), :] = pair
        send_slots(0 + 2, head_send, head_got)
        arrive_slots(2, head_got)

        def rounded(array):
            return array.astype(jnp.bfloat16).astype(jnp.float32)

        cosine = trig_ref[step, 0:1, :]
        sine = trig_ref[step, 1:2, :]

        def turned(heads):
            heads = rounded(heads)
            heads = heads * lax.rsqrt(
                jnp.sum(heads * heads, axis=1, keepdims=True) / HEAD + EPSILON
            )
            return rounded(heads * cosine + pltpu.roll(heads, half, axis=1) * sine)

        even_rows = head_got[pl.ds(own_heads, KVHEADS, stride=2 * SLOT), :]
        odd_rows = head_got[pl.ds(own_heads + SLOT, KVHEADS, stride=2 * SLOT), :]
        fresh_key = turned(jnp.where(lane < half, even_rows, pltpu.roll(odd_rows, half, axis=1)))
        fresh_value = rounded(
            jnp.where(lane < half, pltpu.roll(even_rows, half, axis=1), odd_rows)
        )
        newk_ref[step] = fresh_key
        newv_ref[step] = fresh_value

        @pl.when(step == 0)
        def _():
            loads[3].wait()
            loads[4].wait()

        known = lax.broadcasted_iota(jnp.int32, (2 * group, length), 1) < length_ref[0]
        for g in range(0, KVHEADS, 2):
            heads = jnp.concatenate(
                [
                    head_got[pl.ds((2 * g + d) * SLOT, own_heads), :]
                    for d in range(4)
                ],
                axis=0,
            )
            heads = turned(heads)
            low_part = lax.broadcasted_iota(jnp.int32, heads.shape, 0) < group
            zero = jnp.zeros_like(heads)
            spread = jnp.concatenate(
                [jnp.where(low_part, heads, zero), jnp.where(low_part, zero, heads)], axis=1
            ).astype(jnp.bfloat16)
            columns = pl.ds(g * HEAD, 2 * HEAD)
            scores = lax.dot_general(
                spread,
                keys[:, columns],
                (((1,), (1,)), ((), ())),
                preferred_element_type=jnp.float32,
            )
            weights = jnp.where(known, jnp.exp(scores * (1.0 / math.sqrt(HEAD))), 0.0)
            total = jnp.sum(weights, axis=1, keepdims=True)
            mixed = jnp.dot(
                weights.astype(jnp.bfloat16), values[:, columns], preferred_element_type=jnp.float32
            )
            mixed = jnp.where(low_part, mixed[:, :HEAD], mixed[:, HEAD:])
            for t in range(STEPS):
                k_t = jnp.where(low_part, newk_ref[t, g : g + 1, :], newk_ref[t, g + 1 : g + 2, :])
                v_t = jnp.where(low_part, newv_ref[t, g : g + 1, :], newv_ref[t, g + 1 : g + 2, :])
                fresh = jnp.exp(
                    jnp.sum(heads * k_t, axis=1, keepdims=True) * (1.0 / math.sqrt(HEAD))
                )
                fresh = jnp.where(step >= t, fresh, 0.0)
                total = total + fresh
                mixed = mixed + rounded(fresh) * v_t
            mixed = mixed / total
            for d in range(4):
                mix_send[pl.ds((2 * g + d) * SLOT, own_heads), :] = mixed[
                    d * own_heads : (d + 1) * own_heads
                ]
        send_slots(3, mix_send, mix_got)
        arrive_slots(3, mix_got)
        mixed = jnp.concatenate(
            [mix_got[pl.ds(j, n, stride=SLOT), :] for j in range(own_heads)], axis=1
        ).astype(jnp.bfloat16)
        mid = jnp.dot(mixed, do_ref[...], preferred_element_type=jnp.float32)
        mid = jnp.concatenate([mid, jnp.zeros((n, HEAD - rank), jnp.float32)], axis=1).astype(
            jnp.bfloat16
        )
        mid_send[...] = mid
        mid_got[me] = mid
        exchange(4, lambda peer: mid_send, mid_got)

        @pl.when(step == 0)
        def _():
            loads[5].wait()

        for i in range(chunks // per):
            piece = jnp.dot(
                mixed, wo[:, pl.ds(i * depth, depth)], preferred_element_type=jnp.float32
            )
            for j in range(per):
                wide[pl.ds(i * per + j, n, stride=padded), :] = piece[:, j * HEAD : (j + 1) * HEAD]
        arrive(4, mid_got)
        mid = jnp.sum(mid_got[...].astype(jnp.float32), axis=0).astype(jnp.bfloat16)
        extra = SCALE * lax.dot_general(
            mid[:, :rank], uo_ref[...], (((1,), (1,)), ((), ())), preferred_element_type=jnp.float32
        )
        gap = jnp.zeros((n, half), jnp.float32)
        extra = jnp.where(
            odd == 1,
            jnp.concatenate([gap, extra], axis=1),
            jnp.concatenate([extra, gap], axis=1),
        )
        for j in range(3):
            place = pl.ds(first_chunk + j, n, stride=padded)
            wide[place, :] = wide[place, :] + extra[:, j * HEAD : (j + 1) * HEAD]
        for r in range(n):
            part_send[r] = wide[pl.ds(r * padded, padded), :].astype(jnp.bfloat16)
        part_got[me] = part_send[me]
        exchange(5, lambda peer: part_send.at[peer], part_got)
        arrive(5, part_got)
        out_ref[step] = jnp.sum(part_got[...].astype(jnp.float32), axis=0)[:chunks]
        return carry

    def send_slots(which, source, target):
        target[pl.ds(pl.multiple_of(me * SLOT, SLOT), SLOT), :] = source[
            pl.ds(pl.multiple_of(me * SLOT, SLOT), SLOT), :
        ]

        def send(i, carry):
            peer = lax.rem(me + i, n)
            pltpu.make_async_remote_copy(
                src_ref=source.at[pl.ds(pl.multiple_of(peer * SLOT, SLOT), SLOT), :],
                dst_ref=target.at[pl.ds(pl.multiple_of(me * SLOT, SLOT), SLOT), :],
                send_sem=send_sem.at[which],
                recv_sem=recv_sem.at[which],
                device_id={"fsdp": peer},
                device_id_type=pl.DeviceIdType.MESH,
            ).start()
            return carry

        lax.fori_loop(1, n, send, 0)

    def arrive_slots(which, target):
        whole = target.at[pl.ds(0, (n - 1) * SLOT), :]
        pltpu.make_async_copy(whole, whole, recv_sem.at[which]).wait()
        pltpu.make_async_copy(whole, whole, send_sem.at[which]).wait()

    lax.fori_loop(0, STEPS, step_body, 0)


def per_device(n, *arrays):
    (
        decode_input_rows,
        cached_rotated_keys,
        cached_value_rows,
        lengths,
        base_query_weight,
        base_key_weight,
        base_value_weight,
        base_output_weight,
        query_adapter_down,
        query_adapter_up,
        key_adapter_down,
        key_adapter_up,
        value_adapter_down,
        value_adapter_up,
        output_adapter_down,
        output_adapter_up,
    ) = arrays
    rows_here, steps, width = decode_input_rows.shape
    fits = (
        rows_here == 1
        and n == PIECES
        and base_query_weight.shape[1] == 4 * HEAD
        and base_key_weight.shape[1] * 2 == HEAD
        and query_adapter_down.shape[0] * 2 == 5 * HEAD
        and output_adapter_up.shape[0] * 2 == 5 * HEAD
    )
    if not fits:
        return per_device_plain(*arrays)
    chunks = width // HEAD
    padded = -(-chunks // 16) * 16
    length, kv_width = cached_rotated_keys.shape[1:]
    depth = 4 * HEAD
    rank = query_adapter_down.shape[1]
    half_size = HEAD // 2
    frequency = THETA ** (-2.0 * jnp.arange(half_size, dtype=jnp.float32) / HEAD)
    positions = (lengths[0] + jnp.arange(steps, dtype=jnp.int32)).astype(jnp.float32)
    angles = positions[:, None] * frequency[None, :]
    cosine, sine = jnp.cos(angles), jnp.sin(angles)
    trig = jnp.stack(
        [
            jnp.concatenate([cosine, cosine], axis=1),
            jnp.concatenate([-sine, sine], axis=1),
        ],
        axis=1,
    )
    vmem = pl.BlockSpec(memory_space=pltpu.VMEM)
    anywhere = pl.BlockSpec(memory_space=pl.ANY)
    smem = pl.BlockSpec(memory_space=pltpu.SMEM)
    bf16, f32 = jnp.bfloat16, jnp.float32
    out, new_keys, new_values = pl.pallas_call(
        functools.partial(decode_kernel, n),
        out_shape=(
            jax.ShapeDtypeStruct((steps, chunks, HEAD), f32),
            jax.ShapeDtypeStruct((steps, KVHEADS, HEAD), f32),
            jax.ShapeDtypeStruct((steps, KVHEADS, HEAD), f32),
        ),
        in_specs=[smem, vmem, vmem] + [anywhere] * 6 + [vmem] * 8,
        out_specs=(vmem, vmem, vmem),
        scratch_shapes=[
            pltpu.VMEM((length, kv_width), bf16),
            pltpu.VMEM((length, kv_width), bf16),
            pltpu.VMEM(base_query_weight.shape, bf16),
            pltpu.VMEM(base_key_weight.shape, bf16),
            pltpu.VMEM(base_value_weight.shape, bf16),
            pltpu.VMEM(base_output_weight.shape, bf16),
            pltpu.VMEM((padded, HEAD), bf16),
            pltpu.VMEM((n, padded, HEAD), bf16),
            pltpu.VMEM((n * padded, HEAD), f32),
            pltpu.VMEM((width // depth, n, depth), bf16),
            pltpu.VMEM((n, 4 * rank), bf16),
            pltpu.VMEM((n, n, 4 * rank), bf16),
            pltpu.VMEM((n * SLOT, HEAD), f32),
            pltpu.VMEM((n * SLOT, HEAD), f32),
            pltpu.VMEM((n * SLOT, HEAD), f32),
            pltpu.VMEM((n * SLOT, HEAD), f32),
            pltpu.VMEM((n, HEAD), bf16),
            pltpu.VMEM((n, n, HEAD), bf16),
            pltpu.VMEM((n, padded, HEAD), bf16),
            pltpu.VMEM((n, padded, HEAD), bf16),
            pltpu.SemaphoreType.DMA((6,)),
            pltpu.SemaphoreType.DMA((6,)),
            pltpu.SemaphoreType.DMA((6,)),
        ],
        compiler_params=pltpu.CompilerParams(
            collective_id=0, has_side_effects=True, vmem_limit_bytes=48 * 1024 * 1024
        ),
    )(
        lengths,
        decode_input_rows.astype(f32).reshape(steps, chunks, HEAD),
        trig,
        cached_rotated_keys.reshape(length, kv_width),
        cached_value_rows.reshape(length, kv_width),
        base_query_weight,
        base_key_weight,
        base_value_weight,
        base_output_weight,
        query_adapter_down,
        key_adapter_down,
        value_adapter_down,
        query_adapter_up,
        key_adapter_up,
        value_adapter_up,
        output_adapter_down,
        output_adapter_up,
    )
    return (
        out.reshape(1, steps, width).astype(bf16),
        new_keys.reshape(1, steps, kv_width).astype(bf16),
        new_values.reshape(1, steps, kv_width).astype(bf16),
    )


def solution(mesh):
    placed = (
        P(("job", "fsdp"), None, None),
        P(("job", "fsdp"), None, None),
        P(("job", "fsdp"), None, None),
        P(("job", "fsdp")),
        P(None, "fsdp"),
        P(None, "fsdp"),
        P(None, "fsdp"),
        P("fsdp", None),
        P(("job", "fsdp"), None),
        P(("job", "fsdp"), None),
        P(("job", "fsdp"), None),
        P(("job", "fsdp"), None),
        P(("job", "fsdp"), None),
        P(("job", "fsdp"), None),
        P(("job", "fsdp"), None),
        P(("job", "fsdp"), None),
    )
    return jax.shard_map(
        functools.partial(per_device, mesh.shape["fsdp"]),
        mesh=mesh,
        in_specs=placed,
        out_specs=(
            P(("job", "fsdp"), None, None),
            P(("job", "fsdp"), None, None),
            P(("job", "fsdp"), None, None),
        ),
        check_vma=False,
    )
```

```python
import functools
import math

import jax
import jax.numpy as jnp
from jax import lax
from jax.experimental import pallas as pl
from jax.experimental.pallas import tpu as pltpu
from jax.sharding import PartitionSpec as P

QHEADS = 64
KVHEADS = 8
HEAD = 128
STEPS = 2


SCALE = 2.0
THETA = 1000000.0
EPSILON = 1e-06


def combined_weight_matrix(base, left, right):
    delta = jnp.dot(left, right.T, preferred_element_type=jnp.float32)
    return (base.astype(jnp.float32) + SCALE * delta).astype(jnp.bfloat16)


def rms_rows(values):
    wide = values.astype(jnp.float32)
    return wide * lax.rsqrt(jnp.mean(wide * wide, axis=-1, keepdims=True) + EPSILON)


def rotary(heads, positions):
    half_size = heads.shape[-1] // 2
    frequency = THETA ** (-2.0 * jnp.arange(half_size, dtype=jnp.float32) / heads.shape[-1])
    angles = positions.astype(jnp.float32)[:, None] * frequency[None, :]
    cosine = jnp.cos(angles)[:, None, :]
    sine_part = jnp.sin(angles)[:, None, :]
    first = heads[..., :half_size]
    second = heads[..., half_size:]
    return jnp.concatenate(
        [first * cosine - second * sine_part, second * cosine + first * sine_part], axis=-1
    )


def attend(query_rot, cached_rotated_keys, cached_value_rows, valid, fresh_keys, fresh_values):
    rows_here, length, width = cached_rotated_keys.shape
    groups = width // HEAD
    query = query_rot.reshape(rows_here, groups, -1, HEAD)
    cached_k = cached_rotated_keys.reshape(rows_here, length, groups, HEAD)
    cached_v = cached_value_rows.reshape(rows_here, length, groups, HEAD)
    recent_k = fresh_keys.reshape(rows_here, -1, groups, HEAD)
    recent_v = fresh_values.reshape(rows_here, -1, groups, HEAD)
    scores = jnp.einsum(
        "rgqd,rlgd->rgql", query, cached_k, preferred_element_type=jnp.float32
    ) / math.sqrt(HEAD)
    fresh_scores = jnp.einsum(
        "rgqd,rlgd->rgql", query, recent_k, preferred_element_type=jnp.float32
    ) / math.sqrt(HEAD)
    weights = jnp.where(valid[:, None, None, :], jnp.exp(scores), jnp.float32(0.0))
    fresh_weights = jnp.exp(fresh_scores)
    total = jnp.sum(weights, axis=-1, keepdims=True) + jnp.sum(
        fresh_weights, axis=-1, keepdims=True
    )
    shares = (weights / total).astype(jnp.bfloat16)
    fresh_shares = (fresh_weights / total).astype(jnp.bfloat16)
    mixed = jnp.einsum("rgql,rlgd->rgqd", shares, cached_v, preferred_element_type=jnp.float32)
    mixed = mixed + jnp.einsum(
        "rgql,rlgd->rgqd", fresh_shares, recent_v, preferred_element_type=jnp.float32
    )
    return mixed.reshape(rows_here, -1).astype(jnp.bfloat16)


def per_device_plain(
    decode_input_rows,
    cached_rotated_keys,
    cached_value_rows,
    lengths,
    base_query_weight,
    base_key_weight,
    base_value_weight,
    base_output_weight,
    query_adapter_down,
    query_adapter_up,
    key_adapter_down,
    key_adapter_up,
    value_adapter_down,
    value_adapter_up,
    output_adapter_down,
    output_adapter_up,
):
    expanded_query_down, expanded_key_down, expanded_value_down, complete_output_rows = (
        lax.all_gather(query_adapter_down, "fsdp", axis=0, tiled=True),
        lax.all_gather(key_adapter_down, "fsdp", axis=0, tiled=True),
        lax.all_gather(value_adapter_down, "fsdp", axis=0, tiled=True),
        lax.all_gather(output_adapter_up, "fsdp", axis=0, tiled=True),
    )
    combined_query_weight = combined_weight_matrix(
        base_query_weight, expanded_query_down, query_adapter_up
    )
    combined_key_weight = combined_weight_matrix(base_key_weight, expanded_key_down, key_adapter_up)
    combined_value_weight = combined_weight_matrix(
        base_value_weight, expanded_value_down, value_adapter_up
    )
    combined_output_weight = combined_weight_matrix(
        base_output_weight, output_adapter_down, complete_output_rows
    )
    rows_here = decode_input_rows.shape[0]
    valid = jnp.arange(cached_rotated_keys.shape[1], dtype=jnp.int32)[None, :] < lengths[:, None]
    fresh_keys = []
    fresh_values = []
    results = []
    for step in range(STEPS):
        stream = decode_input_rows[:, step].astype(jnp.float32)
        if step > 0:
            stream = stream + results[-1].astype(jnp.float32)
        normed = rms_rows(stream).astype(jnp.bfloat16)
        gathered = lax.all_gather(normed, "fsdp", axis=0, tiled=True)
        query = jnp.dot(gathered, combined_query_weight, preferred_element_type=jnp.float32).astype(
            jnp.bfloat16
        )
        key = jnp.dot(gathered, combined_key_weight, preferred_element_type=jnp.float32).astype(
            jnp.bfloat16
        )
        value = jnp.dot(gathered, combined_value_weight, preferred_element_type=jnp.float32).astype(
            jnp.bfloat16
        )
        query, key, value = (
            lax.all_to_all(query, "fsdp", split_axis=0, concat_axis=1, tiled=True),
            lax.all_to_all(key, "fsdp", split_axis=0, concat_axis=1, tiled=True),
            lax.all_to_all(value, "fsdp", split_axis=0, concat_axis=1, tiled=True),
        )
        positions = lengths + step
        query_rot = rotary(rms_rows(query.reshape(rows_here, QHEADS, HEAD)), positions).astype(
            jnp.bfloat16
        )
        key_rot = rotary(rms_rows(key.reshape(rows_here, KVHEADS, HEAD)), positions).astype(
            jnp.bfloat16
        )
        fresh_keys.append(key_rot.reshape(rows_here, -1))
        fresh_values.append(value)
        mixed = attend(
            query_rot,
            cached_rotated_keys,
            cached_value_rows,
            valid,
            jnp.stack(fresh_keys, axis=1),
            jnp.stack(fresh_values, axis=1),
        )
        spread = lax.all_to_all(mixed, "fsdp", split_axis=1, concat_axis=0, tiled=True)
        result = lax.psum_scatter(
            jnp.dot(spread, combined_output_weight, preferred_element_type=jnp.float32),
            "fsdp",
            scatter_dimension=0,
            tiled=True,
        )
        results.append(result.astype(jnp.bfloat16))
    return (
        jnp.stack(results, axis=1),
        jnp.stack(fresh_keys, axis=1),
        jnp.stack(fresh_values, axis=1),
    )


SLOT = 8
PIECES = 16


def decode_kernel(
    n,
    length_ref,
    x_ref,
    trig_ref,
    keys_hbm,
    values_hbm,
    wq_hbm,
    wk_hbm,
    wv_hbm,
    wo_hbm,
    dq_hbm,
    dk_hbm,
    dv_hbm,
    uq_hbm,
    uk_hbm,
    uv_hbm,
    do_hbm,
    uo_hbm,
    out_ref,
    newk_ref,
    newv_ref,
    keys,
    values,
    wq,
    wkv,
    wo,
    down,
    up_q,
    up_kv,
    down_o,
    up_o,
    rows_in,
    in_send,
    in_got,
    cols_send,
    cols_got,
    head_send,
    head_got,
    mix_send,
    mix_got,
    part_send,
    part_got,
    block_cols,
    last_send,
    last_got,
    load_sem,
    send_sem,
    recv_sem,
):
    me = lax.axis_index("fsdp")
    chunks = x_ref.shape[2] // HEAD
    rank, share = dq_hbm.shape
    half = HEAD // 2
    own_heads = wq.shape[1] // HEAD
    length = keys.shape[0]
    group = QHEADS // KVHEADS

    loads = [
        pltpu.make_async_copy(source, target, load_sem.at[i])
        for i, (source, target) in enumerate(
            (
                (dq_hbm, down.at[pl.ds(0, rank), :]),
                (dk_hbm, down.at[pl.ds(rank, rank), :]),
                (dv_hbm, down.at[pl.ds(2 * rank, rank), :]),
                (wq_hbm, wq),
                (wk_hbm, wkv.at[pl.ds(0, half), :]),
                (wv_hbm, wkv.at[pl.ds(half, half), :]),
                (uq_hbm, up_q),
                (uk_hbm, up_kv.at[0]),
                (uv_hbm, up_kv.at[1]),
                (keys_hbm, keys),
                (values_hbm, values),
                (do_hbm, down_o),
                (uo_hbm, up_o),
                (wo_hbm, wo),
            )
        )
    ]
    for load in loads:
        load.start()

    barrier = pltpu.get_barrier_semaphore()

    def greet(i, carry):
        pl.semaphore_signal(
            barrier,
            inc=1,
            device_id={"fsdp": lax.rem(me + i, n)},
            device_id_type=pl.DeviceIdType.MESH,
        )
        return carry

    lax.fori_loop(1, n, greet, 0)
    for c in range(chunks):
        rows_in[pl.ds(c, STEPS, stride=chunks), :] = x_ref[
            0, :, c * HEAD : (c + 1) * HEAD
        ].astype(jnp.float32)
    head_send[...] = jnp.zeros_like(head_send)
    down[pl.ds(3 * rank, rank), :] = jnp.zeros((rank, share), jnp.bfloat16)
    mix_send[...] = jnp.zeros_like(mix_send)
    newk_ref[...] = jnp.zeros_like(newk_ref)
    newv_ref[...] = jnp.zeros_like(newv_ref)
    in_send[...] = jnp.zeros_like(in_send)
    last_send[...] = jnp.zeros_like(last_send)
    block_cols[...] = jnp.zeros_like(block_cols)
    out_ref[...] = jnp.zeros_like(out_ref)
    firsts = [5 * (d // 2) + 2 * (d % 2) for d in range(n)]
    for d, first in enumerate(firsts):
        for t in range(STEPS):
            in_send[pl.ds(d * SLOT + 3 * t, 3), :] = rows_in[pl.ds(t * chunks + first, 3), :]
    pl.semaphore_wait(barrier, n - 1)

    def exchange(which, source_of, target):
        def send(i, carry):
            peer = lax.rem(me + i, n)
            pltpu.make_async_remote_copy(
                src_ref=source_of(peer),
                dst_ref=target.at[me],
                send_sem=send_sem.at[which],
                recv_sem=recv_sem.at[which],
                device_id={"fsdp": peer},
                device_id_type=pl.DeviceIdType.MESH,
            ).start()
            return carry

        lax.fori_loop(1, n, send, 0)

    def arrive(which, target):
        whole = target.at[pl.ds(0, n - 1)]
        pltpu.make_async_copy(whole, whole, recv_sem.at[which]).wait()
        pltpu.make_async_copy(whole, whole, send_sem.at[which]).wait()

    odd = lax.rem(me, 2)
    lane = lax.broadcasted_iota(jnp.int32, (KVHEADS, HEAD), 1)

    def step_body(step, carry):
        mine = []
        for j in range(3):
            early = in_got[pl.ds(j, n, stride=SLOT), :]
            late = in_got[pl.ds(3 + j, n, stride=SLOT), :]
            mine.append(jnp.where(step == 0, early, late))
        mine = jnp.concatenate(mine, axis=1)
        mine = jnp.where(odd == 1, mine[:, half : half + share], mine[:, :share])
        stream = mine + block_cols[0]

        @pl.when(step == 0)
        def _():
            for load in loads[:3]:
                load.wait()

        low = lax.dot_general(
            stream.astype(jnp.bfloat16), down[...], (((1,), (1,)), ((), ())), preferred_element_type=jnp.float32
        )
        columns = jnp.concatenate([stream, low[:, : 3 * rank]], axis=1).astype(jnp.bfloat16)
        cols_send[...] = columns
        cols_got[me] = columns
        exchange(1, lambda peer: cols_send, cols_got)
        arrive(1, cols_got)

        @pl.when(step == 0)
        def _():
            for load in loads[3:9]:
                load.wait()

        query = jnp.zeros((n, wq.shape[1]), jnp.float32)
        pair = jnp.zeros((n, HEAD), jnp.float32)
        squares = jnp.zeros((n, 1), jnp.float32)
        for i in range(n // 2):
            features = pl.ds(i * 2 * share, 2 * share)
            left = jnp.concatenate(
                [
                    cols_got[2 * i].astype(jnp.float32)[:, :share],
                    cols_got[2 * i + 1].astype(jnp.float32)[:, :share],
                ],
                axis=1,
            )
            squares = squares + jnp.sum(left * left, axis=1, keepdims=True)
            left = left.astype(jnp.bfloat16)
            query = query + jnp.dot(left, wq[features, :], preferred_element_type=jnp.float32)
            pair = pair + lax.dot_general(
                left,
                wkv[:, features],
                (((1,), (1,)), ((), ())),
                preferred_element_type=jnp.float32,
            )
        inverse = lax.rsqrt(squares / (chunks * HEAD) + EPSILON)
        low = jnp.sum(cols_got[...].astype(jnp.float32), axis=0)[:, share:].astype(jnp.bfloat16)

        def raised(index, factor, rank_dim):
            return SCALE * lax.dot_general(
                low[:, index * rank : (index + 1) * rank],
                factor,
                (((1,), (rank_dim,)), ((), ())),
                preferred_element_type=jnp.float32,
            )

        query = inverse * (query + raised(0, up_q[...], 0))
        pair = inverse * (
            pair + jnp.concatenate([raised(1, up_kv[0], 1), raised(2, up_kv[1], 1)], axis=1)
        )
        for j in range(own_heads):
            head_send[pl.ds(j, n, stride=SLOT), :] = query[:, j * HEAD : (j + 1) * HEAD]
        head_send[pl.ds(own_heads, n, stride=SLOT), :] = pair
        send_slots(0 + 2, head_send, head_got)
        arrive_slots(2, head_got)

        def rounded(array):
            return array.astype(jnp.bfloat16).astype(jnp.float32)

        cosine = trig_ref[step, 0:1, :]
        sine = trig_ref[step, 1:2, :]

        def turned(heads):
            heads = rounded(heads)
            heads = heads * lax.rsqrt(
                jnp.sum(heads * heads, axis=1, keepdims=True) / HEAD + EPSILON
            )
            return rounded(heads * cosine + pltpu.roll(heads, half, axis=1) * sine)

        even_rows = head_got[pl.ds(own_heads, KVHEADS, stride=2 * SLOT), :]
        odd_rows = head_got[pl.ds(own_heads + SLOT, KVHEADS, stride=2 * SLOT), :]
        fresh_key = turned(jnp.where(lane < half, even_rows, pltpu.roll(odd_rows, half, axis=1)))
        fresh_value = rounded(
            jnp.where(lane < half, pltpu.roll(even_rows, half, axis=1), odd_rows)
        )
        newk_ref[step] = fresh_key
        newv_ref[step] = fresh_value

        @pl.when(step == 0)
        def _():
            loads[9].wait()
            loads[10].wait()

        known = lax.broadcasted_iota(jnp.int32, (2 * group, length), 1) < length_ref[0]
        for g in range(0, KVHEADS, 2):
            heads = jnp.concatenate(
                [
                    head_got[pl.ds((2 * g + d) * SLOT, own_heads), :]
                    for d in range(4)
                ],
                axis=0,
            )
            heads = turned(heads)
            low_part = lax.broadcasted_iota(jnp.int32, heads.shape, 0) < group
            zero = jnp.zeros_like(heads)
            spread = jnp.concatenate(
                [jnp.where(low_part, heads, zero), jnp.where(low_part, zero, heads)], axis=1
            ).astype(jnp.bfloat16)
            columns = pl.ds(g * HEAD, 2 * HEAD)
            scores = lax.dot_general(
                spread,
                keys[:, columns],
                (((1,), (1,)), ((), ())),
                preferred_element_type=jnp.float32,
            )
            weights = jnp.where(known, jnp.exp(scores * (1.0 / math.sqrt(HEAD))), 0.0)
            total = jnp.sum(weights, axis=1, keepdims=True)
            mixed = jnp.dot(
                weights.astype(jnp.bfloat16), values[:, columns], preferred_element_type=jnp.float32
            )
            mixed = jnp.where(low_part, mixed[:, :HEAD], mixed[:, HEAD:])
            for t in range(STEPS):
                k_t = jnp.where(low_part, newk_ref[t, g : g + 1, :], newk_ref[t, g + 1 : g + 2, :])
                v_t = jnp.where(low_part, newv_ref[t, g : g + 1, :], newv_ref[t, g + 1 : g + 2, :])
                fresh = jnp.exp(
                    jnp.sum(heads * k_t, axis=1, keepdims=True) * (1.0 / math.sqrt(HEAD))
                )
                fresh = jnp.where(step >= t, fresh, 0.0)
                total = total + fresh
                mixed = mixed + rounded(fresh) * v_t
            mixed = mixed / total
            for d in range(4):
                mix_send[pl.ds((2 * g + d) * SLOT, own_heads), :] = mixed[
                    d * own_heads : (d + 1) * own_heads
                ]
        send_slots(3, mix_send, mix_got)
        arrive_slots(3, mix_got)
        mixed = jnp.concatenate(
            [mix_got[pl.ds(j, n, stride=SLOT), :] for j in range(own_heads)], axis=1
        ).astype(jnp.bfloat16)

        @pl.when(step == 0)
        def _():
            for load in loads[11:]:
                load.wait()

        mid = lax.dot_general(
            mixed, down_o[...], (((1,), (1,)), ((), ())), preferred_element_type=jnp.float32
        )
        for i in range(n // 2):
            piece = jnp.dot(
                mixed, wo[:, pl.ds(i * 2 * share, 2 * share)], preferred_element_type=jnp.float32
            )
            part_send[2 * i] = jnp.concatenate([piece[:, :share], mid], axis=1).astype(jnp.bfloat16)
            part_send[2 * i + 1] = jnp.concatenate([piece[:, share:], mid], axis=1).astype(
                jnp.bfloat16
            )
        part_got[me] = part_send[me]
        exchange(4, lambda peer: part_send.at[peer], part_got)
        arrive(4, part_got)
        summed = jnp.sum(part_got[...].astype(jnp.float32), axis=0)
        block = rounded(
            summed[:, :share]
            + SCALE
            * jnp.dot(
                summed[:, share:].astype(jnp.bfloat16), up_o[...], preferred_element_type=jnp.float32
            )
        )
        block_cols[0] = block
        gap = jnp.zeros((n, half), jnp.float32)
        block = jnp.where(
            odd == 1,
            jnp.concatenate([gap, block], axis=1),
            jnp.concatenate([block, gap], axis=1),
        )
        for j in range(3):
            last_send[pl.ds(3 * step + j, n, stride=SLOT), :] = block[:, j * HEAD : (j + 1) * HEAD]
        return carry

    def send_slots(which, source, target):
        target[pl.ds(pl.multiple_of(me * SLOT, SLOT), SLOT), :] = source[
            pl.ds(pl.multiple_of(me * SLOT, SLOT), SLOT), :
        ]

        def send(i, carry):
            peer = lax.rem(me + i, n)
            pltpu.make_async_remote_copy(
                src_ref=source.at[pl.ds(pl.multiple_of(peer * SLOT, SLOT), SLOT), :],
                dst_ref=target.at[pl.ds(pl.multiple_of(me * SLOT, SLOT), SLOT), :],
                send_sem=send_sem.at[which],
                recv_sem=recv_sem.at[which],
                device_id={"fsdp": peer},
                device_id_type=pl.DeviceIdType.MESH,
            ).start()
            return carry

        lax.fori_loop(1, n, send, 0)

    def arrive_slots(which, target):
        whole = target.at[pl.ds(0, (n - 1) * SLOT), :]
        pltpu.make_async_copy(whole, whole, recv_sem.at[which]).wait()
        pltpu.make_async_copy(whole, whole, send_sem.at[which]).wait()

    send_slots(0, in_send, in_got)
    arrive_slots(0, in_got)
    lax.fori_loop(0, STEPS, step_body, 0)
    send_slots(5, last_send, last_got)
    arrive_slots(5, last_got)
    for d, first in enumerate(firsts):
        for t in range(STEPS):
            place = pl.ds(first, 3)
            out_ref[t, place, :] = (
                out_ref[t, place, :] + last_got[pl.ds(d * SLOT + 3 * t, 3), :]
            )


def per_device(n, *arrays):
    (
        decode_input_rows,
        cached_rotated_keys,
        cached_value_rows,
        lengths,
        base_query_weight,
        base_key_weight,
        base_value_weight,
        base_output_weight,
        query_adapter_down,
        query_adapter_up,
        key_adapter_down,
        key_adapter_up,
        value_adapter_down,
        value_adapter_up,
        output_adapter_down,
        output_adapter_up,
    ) = arrays
    rows_here, steps, width = decode_input_rows.shape
    fits = (
        rows_here == 1
        and n == PIECES
        and base_query_weight.shape[1] == 4 * HEAD
        and base_key_weight.shape[1] * 2 == HEAD
        and query_adapter_down.shape[0] * 2 == 5 * HEAD
        and output_adapter_up.shape[0] * 2 == 5 * HEAD
    )
    if not fits:
        return per_device_plain(*arrays)
    chunks = width // HEAD
    length, kv_width = cached_rotated_keys.shape[1:]
    rank = query_adapter_down.shape[1]
    half_size = HEAD // 2
    frequency = THETA ** (-2.0 * jnp.arange(half_size, dtype=jnp.float32) / HEAD)
    positions = (lengths[0] + jnp.arange(steps, dtype=jnp.int32)).astype(jnp.float32)
    angles = positions[:, None] * frequency[None, :]
    cosine, sine = jnp.cos(angles), jnp.sin(angles)
    trig = jnp.stack(
        [
            jnp.concatenate([cosine, cosine], axis=1),
            jnp.concatenate([-sine, sine], axis=1),
        ],
        axis=1,
    )
    vmem = pl.BlockSpec(memory_space=pltpu.VMEM)
    anywhere = pl.BlockSpec(memory_space=pl.ANY)
    smem = pl.BlockSpec(memory_space=pltpu.SMEM)
    bf16, f32 = jnp.bfloat16, jnp.float32
    out, new_keys, new_values = pl.pallas_call(
        functools.partial(decode_kernel, n),
        out_shape=(
            jax.ShapeDtypeStruct((steps, chunks, HEAD), f32),
            jax.ShapeDtypeStruct((steps, KVHEADS, HEAD), f32),
            jax.ShapeDtypeStruct((steps, KVHEADS, HEAD), f32),
        ),
        in_specs=[smem, vmem, vmem] + [anywhere] * 14,
        out_specs=(vmem, vmem, vmem),
        scratch_shapes=[
            pltpu.VMEM((length, kv_width), bf16),
            pltpu.VMEM((length, kv_width), bf16),
            pltpu.VMEM(base_query_weight.shape, bf16),
            pltpu.VMEM((HEAD, width), bf16),
            pltpu.VMEM(base_output_weight.shape, bf16),
            pltpu.VMEM((4 * rank, width // n), bf16),
            pltpu.VMEM((rank, base_query_weight.shape[1]), bf16),
            pltpu.VMEM((2, half_size, rank), bf16),
            pltpu.VMEM((rank, base_output_weight.shape[0]), bf16),
            pltpu.VMEM((rank, width // n), bf16),
            pltpu.VMEM((steps * chunks, HEAD), f32),
            pltpu.VMEM((n * SLOT, HEAD), f32),
            pltpu.VMEM((n * SLOT, HEAD), f32),
            pltpu.VMEM((n, width // n + 3 * rank), bf16),
            pltpu.VMEM((n, n, width // n + 3 * rank), bf16),
            pltpu.VMEM((n * SLOT, HEAD), f32),
            pltpu.VMEM((n * SLOT, HEAD), f32),
            pltpu.VMEM((n * SLOT, HEAD), f32),
            pltpu.VMEM((n * SLOT, HEAD), f32),
            pltpu.VMEM((n, n, width // n + rank), bf16),
            pltpu.VMEM((n, n, width // n + rank), bf16),
            pltpu.VMEM((1, n, width // n), f32),
            pltpu.VMEM((n * SLOT, HEAD), f32),
            pltpu.VMEM((n * SLOT, HEAD), f32),
            pltpu.SemaphoreType.DMA((14,)),
            pltpu.SemaphoreType.DMA((6,)),
            pltpu.SemaphoreType.DMA((6,)),
        ],
        compiler_params=pltpu.CompilerParams(
            collective_id=0, has_side_effects=True, vmem_limit_bytes=60 * 1024 * 1024
        ),
    )(
        lengths,
        decode_input_rows,
        trig,
        cached_rotated_keys.reshape(length, kv_width),
        cached_value_rows.reshape(length, kv_width),
        base_query_weight,
        base_key_weight.T,
        base_value_weight.T,
        base_output_weight,
        query_adapter_down.T,
        key_adapter_down.T,
        value_adapter_down.T,
        query_adapter_up.T,
        key_adapter_up,
        value_adapter_up,
        output_adapter_down.T,
        output_adapter_up.T,
    )
    return (
        out.reshape(1, steps, width).astype(bf16),
        new_keys.reshape(1, steps, kv_width).astype(bf16),
        new_values.reshape(1, steps, kv_width).astype(bf16),
    )


def solution(mesh):
    placed = (
        P(("job", "fsdp"), None, None),
        P(("job", "fsdp"), None, None),
        P(("job", "fsdp"), None, None),
        P(("job", "fsdp")),
        P(None, "fsdp"),
        P(None, "fsdp"),
        P(None, "fsdp"),
        P("fsdp", None),
        P(("job", "fsdp"), None),
        P(("job", "fsdp"), None),
        P(("job", "fsdp"), None),
        P(("job", "fsdp"), None),
        P(("job", "fsdp"), None),
        P(("job", "fsdp"), None),
        P(("job", "fsdp"), None),
        P(("job", "fsdp"), None),
    )
    return jax.shard_map(
        functools.partial(per_device, mesh.shape["fsdp"]),
        mesh=mesh,
        in_specs=placed,
        out_specs=(
            P(("job", "fsdp"), None, None),
            P(("job", "fsdp"), None, None),
            P(("job", "fsdp"), None, None),
        ),
        check_vma=False,
    )
```

```python
import functools
import math

import jax
import jax.numpy as jnp
from jax import lax
from jax.experimental import pallas as pl
from jax.experimental.pallas import tpu as pltpu
from jax.sharding import PartitionSpec as P

QHEADS = 64
KVHEADS = 8
HEAD = 128
STEPS = 2


SCALE = 2.0
THETA = 1000000.0
EPSILON = 1e-06


def combined_weight_matrix(base, left, right):
    delta = jnp.dot(left, right.T, preferred_element_type=jnp.float32)
    return (base.astype(jnp.float32) + SCALE * delta).astype(jnp.bfloat16)


def rms_rows(values):
    wide = values.astype(jnp.float32)
    return wide * lax.rsqrt(jnp.mean(wide * wide, axis=-1, keepdims=True) + EPSILON)


def rotary(heads, positions):
    half_size = heads.shape[-1] // 2
    frequency = THETA ** (-2.0 * jnp.arange(half_size, dtype=jnp.float32) / heads.shape[-1])
    angles = positions.astype(jnp.float32)[:, None] * frequency[None, :]
    cosine = jnp.cos(angles)[:, None, :]
    sine_part = jnp.sin(angles)[:, None, :]
    first = heads[..., :half_size]
    second = heads[..., half_size:]
    return jnp.concatenate(
        [first * cosine - second * sine_part, second * cosine + first * sine_part], axis=-1
    )


def attend(query_rot, cached_rotated_keys, cached_value_rows, valid, fresh_keys, fresh_values):
    rows_here, length, width = cached_rotated_keys.shape
    groups = width // HEAD
    query = query_rot.reshape(rows_here, groups, -1, HEAD)
    cached_k = cached_rotated_keys.reshape(rows_here, length, groups, HEAD)
    cached_v = cached_value_rows.reshape(rows_here, length, groups, HEAD)
    recent_k = fresh_keys.reshape(rows_here, -1, groups, HEAD)
    recent_v = fresh_values.reshape(rows_here, -1, groups, HEAD)
    scores = jnp.einsum(
        "rgqd,rlgd->rgql", query, cached_k, preferred_element_type=jnp.float32
    ) / math.sqrt(HEAD)
    fresh_scores = jnp.einsum(
        "rgqd,rlgd->rgql", query, recent_k, preferred_element_type=jnp.float32
    ) / math.sqrt(HEAD)
    weights = jnp.where(valid[:, None, None, :], jnp.exp(scores), jnp.float32(0.0))
    fresh_weights = jnp.exp(fresh_scores)
    total = jnp.sum(weights, axis=-1, keepdims=True) + jnp.sum(
        fresh_weights, axis=-1, keepdims=True
    )
    shares = (weights / total).astype(jnp.bfloat16)
    fresh_shares = (fresh_weights / total).astype(jnp.bfloat16)
    mixed = jnp.einsum("rgql,rlgd->rgqd", shares, cached_v, preferred_element_type=jnp.float32)
    mixed = mixed + jnp.einsum(
        "rgql,rlgd->rgqd", fresh_shares, recent_v, preferred_element_type=jnp.float32
    )
    return mixed.reshape(rows_here, -1).astype(jnp.bfloat16)


def per_device_plain(
    decode_input_rows,
    cached_rotated_keys,
    cached_value_rows,
    lengths,
    base_query_weight,
    base_key_weight,
    base_value_weight,
    base_output_weight,
    query_adapter_down,
    query_adapter_up,
    key_adapter_down,
    key_adapter_up,
    value_adapter_down,
    value_adapter_up,
    output_adapter_down,
    output_adapter_up,
):
    expanded_query_down, expanded_key_down, expanded_value_down, complete_output_rows = (
        lax.all_gather(query_adapter_down, "fsdp", axis=0, tiled=True),
        lax.all_gather(key_adapter_down, "fsdp", axis=0, tiled=True),
        lax.all_gather(value_adapter_down, "fsdp", axis=0, tiled=True),
        lax.all_gather(output_adapter_up, "fsdp", axis=0, tiled=True),
    )
    combined_query_weight = combined_weight_matrix(
        base_query_weight, expanded_query_down, query_adapter_up
    )
    combined_key_weight = combined_weight_matrix(base_key_weight, expanded_key_down, key_adapter_up)
    combined_value_weight = combined_weight_matrix(
        base_value_weight, expanded_value_down, value_adapter_up
    )
    combined_output_weight = combined_weight_matrix(
        base_output_weight, output_adapter_down, complete_output_rows
    )
    rows_here = decode_input_rows.shape[0]
    valid = jnp.arange(cached_rotated_keys.shape[1], dtype=jnp.int32)[None, :] < lengths[:, None]
    fresh_keys = []
    fresh_values = []
    results = []
    for step in range(STEPS):
        stream = decode_input_rows[:, step].astype(jnp.float32)
        if step > 0:
            stream = stream + results[-1].astype(jnp.float32)
        normed = rms_rows(stream).astype(jnp.bfloat16)
        gathered = lax.all_gather(normed, "fsdp", axis=0, tiled=True)
        query = jnp.dot(gathered, combined_query_weight, preferred_element_type=jnp.float32).astype(
            jnp.bfloat16
        )
        key = jnp.dot(gathered, combined_key_weight, preferred_element_type=jnp.float32).astype(
            jnp.bfloat16
        )
        value = jnp.dot(gathered, combined_value_weight, preferred_element_type=jnp.float32).astype(
            jnp.bfloat16
        )
        query, key, value = (
            lax.all_to_all(query, "fsdp", split_axis=0, concat_axis=1, tiled=True),
            lax.all_to_all(key, "fsdp", split_axis=0, concat_axis=1, tiled=True),
            lax.all_to_all(value, "fsdp", split_axis=0, concat_axis=1, tiled=True),
        )
        positions = lengths + step
        query_rot = rotary(rms_rows(query.reshape(rows_here, QHEADS, HEAD)), positions).astype(
            jnp.bfloat16
        )
        key_rot = rotary(rms_rows(key.reshape(rows_here, KVHEADS, HEAD)), positions).astype(
            jnp.bfloat16
        )
        fresh_keys.append(key_rot.reshape(rows_here, -1))
        fresh_values.append(value)
        mixed = attend(
            query_rot,
            cached_rotated_keys,
            cached_value_rows,
            valid,
            jnp.stack(fresh_keys, axis=1),
            jnp.stack(fresh_values, axis=1),
        )
        spread = lax.all_to_all(mixed, "fsdp", split_axis=1, concat_axis=0, tiled=True)
        result = lax.psum_scatter(
            jnp.dot(spread, combined_output_weight, preferred_element_type=jnp.float32),
            "fsdp",
            scatter_dimension=0,
            tiled=True,
        )
        results.append(result.astype(jnp.bfloat16))
    return (
        jnp.stack(results, axis=1),
        jnp.stack(fresh_keys, axis=1),
        jnp.stack(fresh_values, axis=1),
    )


SLOT = 8
PIECES = 16


def decode_kernel(
    n,
    length_ref,
    x_ref,
    trig_ref,
    keys_hbm,
    values_hbm,
    wq_hbm,
    wk_hbm,
    wv_hbm,
    wo_hbm,
    dq_hbm,
    dk_hbm,
    dv_hbm,
    uq_hbm,
    uk_hbm,
    uv_hbm,
    do_hbm,
    uo_hbm,
    out_ref,
    newk_ref,
    newv_ref,
    keys,
    values,
    wq,
    wkv,
    wo,
    down,
    up_q,
    up_kv,
    down_o,
    up_o,
    rows_in,
    in_send,
    in_got,
    cols_send,
    cols_got,
    head_send,
    head_got,
    mix_send,
    mix_got,
    part_send,
    part_got,
    block_cols,
    last_send,
    last_got,
    load_sem,
    send_sem,
    recv_sem,
    cols_sem,
):
    me = lax.axis_index("fsdp")
    chunks = x_ref.shape[2] // HEAD
    rank, share = dq_hbm.shape
    half = HEAD // 2
    own_heads = wq.shape[1] // HEAD
    length = keys.shape[0]
    group = QHEADS // KVHEADS

    loads = [
        pltpu.make_async_copy(source, target, load_sem.at[i])
        for i, (source, target) in enumerate(
            (
                (dq_hbm, down.at[pl.ds(0, rank), :]),
                (dk_hbm, down.at[pl.ds(rank, rank), :]),
                (dv_hbm, down.at[pl.ds(2 * rank, rank), :]),
                (wq_hbm, wq),
                (wk_hbm, wkv.at[pl.ds(0, half), :]),
                (wv_hbm, wkv.at[pl.ds(half, half), :]),
                (uq_hbm, up_q),
                (uk_hbm, up_kv.at[0]),
                (uv_hbm, up_kv.at[1]),
                (keys_hbm, keys),
                (values_hbm, values),
                (do_hbm, down_o),
                (uo_hbm, up_o),
                (wo_hbm, wo),
            )
        )
    ]
    for load in loads:
        load.start()

    barrier = pltpu.get_barrier_semaphore()

    def greet(i, carry):
        pl.semaphore_signal(
            barrier,
            inc=1,
            device_id={"fsdp": lax.rem(me + i, n)},
            device_id_type=pl.DeviceIdType.MESH,
        )
        return carry

    lax.fori_loop(1, n, greet, 0)
    for c in range(chunks):
        rows_in[pl.ds(c, STEPS, stride=chunks), :] = x_ref[
            0, :, c * HEAD : (c + 1) * HEAD
        ].astype(jnp.float32)
    head_send[...] = jnp.zeros_like(head_send)
    down[pl.ds(3 * rank, rank), :] = jnp.zeros((rank, share), jnp.bfloat16)
    mix_send[...] = jnp.zeros_like(mix_send)
    newk_ref[...] = jnp.zeros_like(newk_ref)
    newv_ref[...] = jnp.zeros_like(newv_ref)
    in_send[...] = jnp.zeros_like(in_send)
    last_send[...] = jnp.zeros_like(last_send)
    block_cols[...] = jnp.zeros_like(block_cols)
    out_ref[...] = jnp.zeros_like(out_ref)
    firsts = [5 * (d // 2) + 2 * (d % 2) for d in range(n)]
    for d, first in enumerate(firsts):
        for t in range(STEPS):
            in_send[pl.ds(d * SLOT + 3 * t, 3), :] = rows_in[pl.ds(t * chunks + first, 3), :]
    pl.semaphore_wait(barrier, n - 1)

    def arrive(which, target):
        whole = target.at[pl.ds(0, n - 1)]
        pltpu.make_async_copy(whole, whole, recv_sem.at[which]).wait()
        pltpu.make_async_copy(whole, whole, send_sem.at[which]).wait()

    odd = lax.rem(me, 2)
    own_pair = me // 2
    sibling = me + 1 - 2 * odd
    lane = lax.broadcasted_iota(jnp.int32, (KVHEADS, HEAD), 1)

    def step_body(step, carry):
        mine = []
        for j in range(3):
            early = in_got[pl.ds(j, n, stride=SLOT), :]
            late = in_got[pl.ds(3 + j, n, stride=SLOT), :]
            mine.append(jnp.where(step == 0, early, late))
        mine = jnp.concatenate(mine, axis=1)
        mine = jnp.where(odd == 1, mine[:, half : half + share], mine[:, :share])
        stream = mine + block_cols[0]

        @pl.when(step == 0)
        def _():
            for load in loads[:3]:
                load.wait()

        low = lax.dot_general(
            stream.astype(jnp.bfloat16), down[...], (((1,), (1,)), ((), ())), preferred_element_type=jnp.float32
        )
        columns = jnp.concatenate([stream, low[:, : 3 * rank]], axis=1).astype(jnp.bfloat16)
        cols_send[...] = columns
        cols_got[me] = columns

        def send_columns(i, carry):
            peer = lax.rem(me + i, n)
            pltpu.make_async_remote_copy(
                src_ref=cols_send,
                dst_ref=cols_got.at[me],
                send_sem=send_sem.at[1],
                recv_sem=cols_sem.at[me],
                device_id={"fsdp": peer},
                device_id_type=pl.DeviceIdType.MESH,
            ).start()
            return carry

        lax.fori_loop(1, n, send_columns, 0)

        @pl.when(step == 0)
        def _():
            for load in loads[3:9]:
                load.wait()

        query = jnp.zeros((n, wq.shape[1]), jnp.float32)
        pair = jnp.zeros((n, HEAD), jnp.float32)
        squares = jnp.zeros((n, 1), jnp.float32)
        for i in range(n // 2):
            both = lax.rem(own_pair + i, n // 2)
            for sender in (sibling,) if i == 0 else (2 * both, 2 * both + 1):
                landed = cols_got.at[sender]
                pltpu.make_async_copy(landed, landed, cols_sem.at[sender]).wait()
            features = pl.ds(pl.multiple_of(both * 2 * share, 2 * share), 2 * share)
            left = jnp.concatenate(
                [
                    cols_got[2 * both].astype(jnp.float32)[:, :share],
                    cols_got[2 * both + 1].astype(jnp.float32)[:, :share],
                ],
                axis=1,
            )
            squares = squares + jnp.sum(left * left, axis=1, keepdims=True)
            left = left.astype(jnp.bfloat16)
            query = query + jnp.dot(left, wq[features, :], preferred_element_type=jnp.float32)
            pair = pair + lax.dot_general(
                left,
                wkv[:, features],
                (((1,), (1,)), ((), ())),
                preferred_element_type=jnp.float32,
            )
        sent = cols_got.at[pl.ds(0, n - 1)]
        pltpu.make_async_copy(sent, sent, send_sem.at[1]).wait()
        inverse = lax.rsqrt(squares / (chunks * HEAD) + EPSILON)
        low = jnp.sum(cols_got[...].astype(jnp.float32), axis=0)[:, share:].astype(jnp.bfloat16)

        def raised(index, factor, rank_dim):
            return SCALE * lax.dot_general(
                low[:, index * rank : (index + 1) * rank],
                factor,
                (((1,), (rank_dim,)), ((), ())),
                preferred_element_type=jnp.float32,
            )

        query = inverse * (query + raised(0, up_q[...], 0))
        pair = inverse * (
            pair + jnp.concatenate([raised(1, up_kv[0], 1), raised(2, up_kv[1], 1)], axis=1)
        )
        for j in range(own_heads):
            head_send[pl.ds(j, n, stride=SLOT), :] = query[:, j * HEAD : (j + 1) * HEAD]
        head_send[pl.ds(own_heads, n, stride=SLOT), :] = pair
        send_slots(0 + 2, head_send, head_got)
        arrive_slots(2, head_got)

        def rounded(array):
            return array.astype(jnp.bfloat16).astype(jnp.float32)

        cosine = trig_ref[step, 0:1, :]
        sine = trig_ref[step, 1:2, :]

        def turned(heads):
            heads = rounded(heads)
            heads = heads * lax.rsqrt(
                jnp.sum(heads * heads, axis=1, keepdims=True) / HEAD + EPSILON
            )
            return rounded(heads * cosine + pltpu.roll(heads, half, axis=1) * sine)

        even_rows = head_got[pl.ds(own_heads, KVHEADS, stride=2 * SLOT), :]
        odd_rows = head_got[pl.ds(own_heads + SLOT, KVHEADS, stride=2 * SLOT), :]
        fresh_key = turned(jnp.where(lane < half, even_rows, pltpu.roll(odd_rows, half, axis=1)))
        fresh_value = rounded(
            jnp.where(lane < half, pltpu.roll(even_rows, half, axis=1), odd_rows)
        )
        newk_ref[step] = fresh_key
        newv_ref[step] = fresh_value

        @pl.when(step == 0)
        def _():
            loads[9].wait()
            loads[10].wait()

        known = lax.broadcasted_iota(jnp.int32, (2 * group, length), 1) < length_ref[0]
        for g in range(0, KVHEADS, 2):
            heads = jnp.concatenate(
                [
                    head_got[pl.ds((2 * g + d) * SLOT, own_heads), :]
                    for d in range(4)
                ],
                axis=0,
            )
            heads = turned(heads)
            low_part = lax.broadcasted_iota(jnp.int32, heads.shape, 0) < group
            zero = jnp.zeros_like(heads)
            spread = jnp.concatenate(
                [jnp.where(low_part, heads, zero), jnp.where(low_part, zero, heads)], axis=1
            ).astype(jnp.bfloat16)
            columns = pl.ds(g * HEAD, 2 * HEAD)
            scores = lax.dot_general(
                spread,
                keys[:, columns],
                (((1,), (1,)), ((), ())),
                preferred_element_type=jnp.float32,
            )
            weights = jnp.where(known, jnp.exp(scores * (1.0 / math.sqrt(HEAD))), 0.0)
            total = jnp.sum(weights, axis=1, keepdims=True)
            mixed = jnp.dot(
                weights.astype(jnp.bfloat16), values[:, columns], preferred_element_type=jnp.float32
            )
            mixed = jnp.where(low_part, mixed[:, :HEAD], mixed[:, HEAD:])
            for t in range(STEPS):
                k_t = jnp.where(low_part, newk_ref[t, g : g + 1, :], newk_ref[t, g + 1 : g + 2, :])
                v_t = jnp.where(low_part, newv_ref[t, g : g + 1, :], newv_ref[t, g + 1 : g + 2, :])
                fresh = jnp.exp(
                    jnp.sum(heads * k_t, axis=1, keepdims=True) * (1.0 / math.sqrt(HEAD))
                )
                fresh = jnp.where(step >= t, fresh, 0.0)
                total = total + fresh
                mixed = mixed + rounded(fresh) * v_t
            mixed = mixed / total
            for d in range(4):
                mix_send[pl.ds((2 * g + d) * SLOT, own_heads), :] = mixed[
                    d * own_heads : (d + 1) * own_heads
                ]
        send_slots(3, mix_send, mix_got)
        arrive_slots(3, mix_got)
        mixed = jnp.concatenate(
            [mix_got[pl.ds(j, n, stride=SLOT), :] for j in range(own_heads)], axis=1
        ).astype(jnp.bfloat16)

        @pl.when(step == 0)
        def _():
            for load in loads[11:]:
                load.wait()

        mid = lax.dot_general(
            mixed, down_o[...], (((1,), (1,)), ((), ())), preferred_element_type=jnp.float32
        )
        for i in range(1, n // 2 + 1):
            both = lax.rem(own_pair + i, n // 2)
            piece = jnp.dot(
                mixed,
                wo[:, pl.ds(pl.multiple_of(both * 2 * share, 2 * share), 2 * share)],
                preferred_element_type=jnp.float32,
            )
            part_send[2 * both] = jnp.concatenate([piece[:, :share], mid], axis=1).astype(
                jnp.bfloat16
            )
            part_send[2 * both + 1] = jnp.concatenate([piece[:, share:], mid], axis=1).astype(
                jnp.bfloat16
            )
            for peer in (sibling,) if i == n // 2 else (2 * both, 2 * both + 1):
                pltpu.make_async_remote_copy(
                    src_ref=part_send.at[peer],
                    dst_ref=part_got.at[me],
                    send_sem=send_sem.at[4],
                    recv_sem=recv_sem.at[4],
                    device_id={"fsdp": peer},
                    device_id_type=pl.DeviceIdType.MESH,
                ).start()
        part_got[me] = part_send[me]
        arrive(4, part_got)
        summed = jnp.sum(part_got[...].astype(jnp.float32), axis=0)
        block = rounded(
            summed[:, :share]
            + SCALE
            * jnp.dot(
                summed[:, share:].astype(jnp.bfloat16), up_o[...], preferred_element_type=jnp.float32
            )
        )
        block_cols[0] = block
        gap = jnp.zeros((n, half), jnp.float32)
        block = jnp.where(
            odd == 1,
            jnp.concatenate([gap, block], axis=1),
            jnp.concatenate([block, gap], axis=1),
        )
        for j in range(3):
            last_send[pl.ds(3 * step + j, n, stride=SLOT), :] = block[:, j * HEAD : (j + 1) * HEAD]
        return carry

    def send_slots(which, source, target):
        target[pl.ds(pl.multiple_of(me * SLOT, SLOT), SLOT), :] = source[
            pl.ds(pl.multiple_of(me * SLOT, SLOT), SLOT), :
        ]

        def send(i, carry):
            peer = lax.rem(me + i, n)
            pltpu.make_async_remote_copy(
                src_ref=source.at[pl.ds(pl.multiple_of(peer * SLOT, SLOT), SLOT), :],
                dst_ref=target.at[pl.ds(pl.multiple_of(me * SLOT, SLOT), SLOT), :],
                send_sem=send_sem.at[which],
                recv_sem=recv_sem.at[which],
                device_id={"fsdp": peer},
                device_id_type=pl.DeviceIdType.MESH,
            ).start()
            return carry

        lax.fori_loop(1, n, send, 0)

    def arrive_slots(which, target):
        whole = target.at[pl.ds(0, (n - 1) * SLOT), :]
        pltpu.make_async_copy(whole, whole, recv_sem.at[which]).wait()
        pltpu.make_async_copy(whole, whole, send_sem.at[which]).wait()

    send_slots(0, in_send, in_got)
    arrive_slots(0, in_got)
    lax.fori_loop(0, STEPS, step_body, 0)
    send_slots(5, last_send, last_got)
    arrive_slots(5, last_got)
    for d, first in enumerate(firsts):
        for t in range(STEPS):
            place = pl.ds(first, 3)
            out_ref[t, place, :] = (
                out_ref[t, place, :] + last_got[pl.ds(d * SLOT + 3 * t, 3), :]
            )


def per_device(n, *arrays):
    (
        decode_input_rows,
        cached_rotated_keys,
        cached_value_rows,
        lengths,
        base_query_weight,
        base_key_weight,
        base_value_weight,
        base_output_weight,
        query_adapter_down,
        query_adapter_up,
        key_adapter_down,
        key_adapter_up,
        value_adapter_down,
        value_adapter_up,
        output_adapter_down,
        output_adapter_up,
    ) = arrays
    rows_here, steps, width = decode_input_rows.shape
    fits = (
        rows_here == 1
        and n == PIECES
        and base_query_weight.shape[1] == 4 * HEAD
        and base_key_weight.shape[1] * 2 == HEAD
        and query_adapter_down.shape[0] * 2 == 5 * HEAD
        and output_adapter_up.shape[0] * 2 == 5 * HEAD
    )
    if not fits:
        return per_device_plain(*arrays)
    chunks = width // HEAD
    length, kv_width = cached_rotated_keys.shape[1:]
    rank = query_adapter_down.shape[1]
    half_size = HEAD // 2
    frequency = THETA ** (-2.0 * jnp.arange(half_size, dtype=jnp.float32) / HEAD)
    positions = (lengths[0] + jnp.arange(steps, dtype=jnp.int32)).astype(jnp.float32)
    angles = positions[:, None] * frequency[None, :]
    cosine, sine = jnp.cos(angles), jnp.sin(angles)
    trig = jnp.stack(
        [
            jnp.concatenate([cosine, cosine], axis=1),
            jnp.concatenate([-sine, sine], axis=1),
        ],
        axis=1,
    )
    vmem = pl.BlockSpec(memory_space=pltpu.VMEM)
    anywhere = pl.BlockSpec(memory_space=pl.ANY)
    smem = pl.BlockSpec(memory_space=pltpu.SMEM)
    bf16, f32 = jnp.bfloat16, jnp.float32
    out, new_keys, new_values = pl.pallas_call(
        functools.partial(decode_kernel, n),
        out_shape=(
            jax.ShapeDtypeStruct((steps, chunks, HEAD), f32),
            jax.ShapeDtypeStruct((steps, KVHEADS, HEAD), f32),
            jax.ShapeDtypeStruct((steps, KVHEADS, HEAD), f32),
        ),
        in_specs=[smem, vmem, vmem] + [anywhere] * 14,
        out_specs=(vmem, vmem, vmem),
        scratch_shapes=[
            pltpu.VMEM((length, kv_width), bf16),
            pltpu.VMEM((length, kv_width), bf16),
            pltpu.VMEM(base_query_weight.shape, bf16),
            pltpu.VMEM((HEAD, width), bf16),
            pltpu.VMEM(base_output_weight.shape, bf16),
            pltpu.VMEM((4 * rank, width // n), bf16),
            pltpu.VMEM((rank, base_query_weight.shape[1]), bf16),
            pltpu.VMEM((2, half_size, rank), bf16),
            pltpu.VMEM((rank, base_output_weight.shape[0]), bf16),
            pltpu.VMEM((rank, width // n), bf16),
            pltpu.VMEM((steps * chunks, HEAD), f32),
            pltpu.VMEM((n * SLOT, HEAD), f32),
            pltpu.VMEM((n * SLOT, HEAD), f32),
            pltpu.VMEM((n, width // n + 3 * rank), bf16),
            pltpu.VMEM((n, n, width // n + 3 * rank), bf16),
            pltpu.VMEM((n * SLOT, HEAD), f32),
            pltpu.VMEM((n * SLOT, HEAD), f32),
            pltpu.VMEM((n * SLOT, HEAD), f32),
            pltpu.VMEM((n * SLOT, HEAD), f32),
            pltpu.VMEM((n, n, width // n + rank), bf16),
            pltpu.VMEM((n, n, width // n + rank), bf16),
            pltpu.VMEM((1, n, width // n), f32),
            pltpu.VMEM((n * SLOT, HEAD), f32),
            pltpu.VMEM((n * SLOT, HEAD), f32),
            pltpu.SemaphoreType.DMA((14,)),
            pltpu.SemaphoreType.DMA((6,)),
            pltpu.SemaphoreType.DMA((6,)),
            pltpu.SemaphoreType.DMA((n,)),
        ],
        compiler_params=pltpu.CompilerParams(
            collective_id=0, has_side_effects=True, vmem_limit_bytes=60 * 1024 * 1024
        ),
    )(
        lengths,
        decode_input_rows,
        trig,
        cached_rotated_keys.reshape(length, kv_width),
        cached_value_rows.reshape(length, kv_width),
        base_query_weight,
        base_key_weight.T,
        base_value_weight.T,
        base_output_weight,
        query_adapter_down.T,
        key_adapter_down.T,
        value_adapter_down.T,
        query_adapter_up.T,
        key_adapter_up,
        value_adapter_up,
        output_adapter_down.T,
        output_adapter_up.T,
    )
    return (
        out.reshape(1, steps, width).astype(bf16),
        new_keys.reshape(1, steps, kv_width).astype(bf16),
        new_values.reshape(1, steps, kv_width).astype(bf16),
    )


def solution(mesh):
    placed = (
        P(("job", "fsdp"), None, None),
        P(("job", "fsdp"), None, None),
        P(("job", "fsdp"), None, None),
        P(("job", "fsdp")),
        P(None, "fsdp"),
        P(None, "fsdp"),
        P(None, "fsdp"),
        P("fsdp", None),
        P(("job", "fsdp"), None),
        P(("job", "fsdp"), None),
        P(("job", "fsdp"), None),
        P(("job", "fsdp"), None),
        P(("job", "fsdp"), None),
        P(("job", "fsdp"), None),
        P(("job", "fsdp"), None),
        P(("job", "fsdp"), None),
    )
    return jax.shard_map(
        functools.partial(per_device, mesh.shape["fsdp"]),
        mesh=mesh,
        in_specs=placed,
        out_specs=(
            P(("job", "fsdp"), None, None),
            P(("job", "fsdp"), None, None),
            P(("job", "fsdp"), None, None),
        ),
        check_vma=False,
    )
```
